32 devices in a mesh: obs: 2 (over x), chan: 16 (over z, y, core).
Axes of the slice: x: 2, y: 2, z: 4, core: 2. Of those that a mesh axis runs over, the one named last changes fastest.
Arguments:
- voltages: bfloat16 [2, 1024, 512, 256], P(None, ('obs', 'chan')), parts along dimension 1, may hold values from -6 to 6
- cal_gains: int32 [2, 1024, 512], P(None, ('obs', 'chan')), parts along dimension 1, may hold values from -65536 to 65536
- beam_phase: int32 [512, 512], replicated, may hold values from 0 to 1023
- delays: int32 [128, 512], replicated, may hold values from 0 to 255
Outputs:
- dedispersed: float32 [1024, 128, 256], P(('obs', 'chan')), parts along dimension 0
The draws below stay inside these ranges and needn't reach their ends.
There are 2 independent parts, one for each index of `obs`. The reference program is written for one: setup_inputs(seed, part) draws one part's arguments, and reference() takes and returns one part's arrays. A program takes and returns all parts, laid end to end along the dimension named above; an argument that names none is the same for every part. Nothing has to cross between parts.
All inputs are finite; a program needn't handle non-finite values.
Results may differ from the reference program's by a relative error of at most 0.0071.
Values may be sent and summed in bfloat16 or wider, within the bound.
A program may use at most 192 MiB of HBM per device.

```python
import math
import jax
import jax.numpy as jnp
from jax import lax

STATIONS = 512
CHANNELS = 512
BEAMS = 512
TRIALS = 128
TIME = 256
PHASES = 1024


def with_ends(array, stream_key, least, top_value):
    spot = [jax.random.randint(jax.random.fold_in(stream_key, axis), (), 0, length) for axis, length in enumerate(array.shape)]
    longest = array.shape.index(max(array.shape))
    next_to = spot[:longest] + [(spot[longest] + 1) % array.shape[longest]] + spot[longest + 1:]
    return array.at[tuple(spot)].set(least).at[tuple(next_to)].set(top_value)


def block_scale(key, extent, pieces, low, top_value):
    def one(dim, parts):
        draws = jax.random.uniform(jax.random.fold_in(jax.random.fold_in(key, 6), dim), (parts,), jnp.float32, low / len(pieces), top_value / len(pieces))
        return jnp.repeat(jnp.exp(draws), extent[dim] // parts).reshape((-1,) + (1,) * (len(extent) - dim - 1))

    level = one(*pieces[0])
    for cut in pieces[1:]:
        level = level * one(*cut)
    return level


def scatter_about(rng, shape, scale, limit, split=(), kind=jnp.bfloat16):
    gain = block_scale(rng, shape, split, -0.22, 0.18) if split else 1.0
    array = jax.random.normal(rng, shape, jnp.float32) * scale * gain
    return jnp.minimum(jnp.maximum(array, -limit), limit).astype(kind)


def setup_inputs(seed: int = 0, part: int = 0) -> dict:
    keys = jax.random.split(jax.random.key(seed), 5)
    part_splits = jax.random.split(jax.random.fold_in(keys[4], part), 5)
    return {
        "voltages": scatter_about(part_splits[0], (2, STATIONS, CHANNELS, TIME), 1.0, 6.0, ((1, 16),)),
        "cal_gains": with_ends(jax.random.randint(part_splits[1], (2, STATIONS, CHANNELS), -65536, 65537), jax.random.fold_in(part_splits[1], 1), -65536, 65536).astype(jnp.int32),
        "beam_phase": with_ends(jax.random.randint(keys[2], (BEAMS, STATIONS), 0, PHASES), jax.random.fold_in(keys[2], 1), 0, PHASES - 1).astype(jnp.int32),
        "delays": with_ends(jax.random.randint(keys[3], (TRIALS, CHANNELS), 0, TIME), jax.random.fold_in(keys[3], 1), 0, TIME - 1).astype(jnp.int32),
    }


def reference(voltages, cal_gains, beam_phase, delays):
    gains = cal_gains.astype(jnp.float32) / 65536.0
    gain_real = gains[0][:, :, None]
    gain_imag = gains[1][:, :, None]
    volt_real = voltages[0].astype(jnp.float32)
    volt_imag = voltages[1].astype(jnp.float32)
    cal_real = (volt_real * gain_real - volt_imag * gain_imag).astype(jnp.bfloat16)
    cal_imag = (volt_real * gain_imag + volt_imag * gain_real).astype(jnp.bfloat16)
    stacked = jnp.concatenate([cal_real, cal_imag], axis=0)
    angles = beam_phase.astype(jnp.float32) * (2.0 * math.pi / PHASES)
    scaling = 1.0 / math.sqrt(STATIONS)
    real_part = jnp.cos(angles) * scaling
    imag_part = jnp.sin(angles) * scaling
    upper_rows = jnp.concatenate([real_part, -imag_part], axis=1)
    bottom = jnp.concatenate([imag_part, real_part], axis=1)
    weights = jnp.concatenate([upper_rows, bottom], axis=0).astype(jnp.bfloat16)
    per_group = 8
    grouped = stacked.reshape(2 * STATIONS, CHANNELS // per_group, per_group, TIME)
    grouped = jnp.transpose(grouped, (1, 0, 2, 3))

    def detect_group(received):
        flattened = received.reshape(2 * STATIONS, per_group * TIME)
        beam_sum = jnp.dot(weights, flattened, preferred_element_type=jnp.float32)
        powers = beam_sum[:BEAMS] ** 2 + beam_sum[BEAMS:] ** 2
        return powers.reshape(BEAMS, per_group, TIME).astype(jnp.bfloat16)
    powers = lax.map(detect_group, grouped)
    powers = jnp.transpose(powers, (1, 0, 2, 3)).reshape(BEAMS, CHANNELS, TIME)
    series = powers.astype(jnp.float32)
    centred = series - lax.optimization_barrier(jnp.mean(series, axis=2, keepdims=True))
    sample_index = jnp.arange(TIME, dtype=jnp.int32)

    def one_trial(delay_row):
        shifted = (sample_index[None, :] + delay_row.astype(jnp.int32)[:, None]) % TIME
        shifted = jnp.broadcast_to(shifted[None], centred.shape)
        picked = jnp.take_along_axis(centred, shifted, axis=2)
        return lax.optimization_barrier(jnp.sum(picked, axis=1)) / math.sqrt(CHANNELS)
    trials_out = lax.map(one_trial, delays)
    return jnp.transpose(trials_out, (1, 0, 2))
```

```python
import functools
import math

import jax
import jax.numpy as jnp
import numpy as np
from jax import lax
from jax.experimental import pallas as pl
from jax.experimental.pallas import tpu as pltpu
from jax.sharding import PartitionSpec as P

PHASES = 1024
CHUNKS = 4


def beam_matrix(beam_phase, group_count, own_half):
    beam_count, station_count = beam_phase.shape
    half = group_count // 2
    local_beams = beam_count // group_count
    grid = beam_phase.reshape(2, half, local_beams, station_count)
    grid = jnp.where(own_half == 0, grid[::-1], grid)
    grid = jnp.transpose(grid, (1, 0, 2, 3)).reshape(beam_count, group_count, station_count // group_count)
    angles = grid.astype(jnp.float32) * (2.0 * math.pi / PHASES)
    scaling = 1.0 / math.sqrt(station_count)
    real_part = jnp.cos(angles) * scaling
    imag_part = jnp.sin(angles) * scaling
    upper_rows = jnp.stack([real_part, -imag_part], axis=2)
    bottom = jnp.stack([imag_part, real_part], axis=2)
    rows = jnp.concatenate([upper_rows, bottom], axis=0)
    return rows.reshape(2 * beam_count, 2 * station_count).astype(jnp.bfloat16)


def beam_kernel(weight_ref, table_ref, data_ref, out_ref):
    rows = weight_ref.shape[1]
    beams = weight_ref.shape[0] // 2
    data = data_ref[:, 0].reshape(rows, data_ref.shape[3])
    sums = jnp.dot(weight_ref[...], data, preferred_element_type=jnp.float32)
    powers = (sums[:beams] * sums[:beams] + sums[beams:] * sums[beams:]).astype(jnp.bfloat16)
    spectrum = jnp.dot(powers, table_ref[...], preferred_element_type=jnp.float32)
    out_ref[:, 0] = spectrum.astype(jnp.bfloat16).reshape(out_ref.shape[0], out_ref.shape[2], out_ref.shape[3])


def detect_spectra(weights, table, received):
    group_count, items, rows, time_count = received.shape
    beams = weights.shape[0] // 2
    half = group_count // 2
    return pl.pallas_call(
        beam_kernel,
        grid=(items,),
        out_shape=jax.ShapeDtypeStruct((half, items, beams // half, time_count), jnp.bfloat16),
        in_specs=[
            pl.BlockSpec(weights.shape, lambda c: (0, 0)),
            pl.BlockSpec(table.shape, lambda c: (0, 0)),
            pl.BlockSpec((group_count, 1, rows, time_count), lambda c: (0, c, 0, 0)),
        ],
        out_specs=pl.BlockSpec((half, 1, beams // half, time_count), lambda c: (0, c, 0, 0)),
        compiler_params=pltpu.CompilerParams(vmem_limit_bytes=32 * 2**20),
        cost_estimate=pl.CostEstimate(
            flops=2 * items * time_count * (weights.size + beams * time_count),
            bytes_accessed=2 * (received.size + weights.size + items * beams * time_count),
            transcendentals=0,
        ),
    )(weights, table, received)


def rotations(delays, time_count):
    freqs = time_count // 2
    low = min(16, freqs)
    high = freqs // low
    turned = delays.T

    def unit(multiples):
        level = multiples[:, None, None] * turned[None] % time_count
        angle = level.astype(jnp.float32) * (2.0 * math.pi / time_count)
        return jnp.cos(angle), jnp.sin(angle)

    low_cos, low_sin = unit(jnp.arange(1, low + 1, dtype=jnp.int32))
    high_cos, high_sin = unit(jnp.arange(high, dtype=jnp.int32) * low)
    cosine = high_cos[:, None] * low_cos[None] - high_sin[:, None] * low_sin[None]
    sine = high_cos[:, None] * low_sin[None] + high_sin[:, None] * low_cos[None]
    cosine = cosine.reshape((freqs,) + turned.shape).astype(jnp.bfloat16)
    sine = sine.reshape((freqs,) + turned.shape).astype(jnp.bfloat16)
    return jnp.concatenate(
        [jnp.concatenate([cosine, sine], axis=2), jnp.concatenate([-sine, cosine], axis=2)], axis=1
    )


def body(voltages, cal_gains, beam_phase, delays):
    group_count = lax.axis_size("chan")
    half = group_count // 2
    me = lax.axis_index("chan")
    own_half = me // half
    _, stations, channels, time_count = voltages.shape
    items = channels // group_count // CHUNKS
    freqs = time_count // 2
    trials = delays.shape[0]
    local_beams = beam_phase.shape[0] // group_count

    weights = beam_matrix(beam_phase, group_count, own_half)
    turn = np.outer(np.arange(time_count), np.arange(1, freqs + 1)) % time_count
    turn = turn * (2.0 * np.pi / time_count)
    table = jnp.asarray(np.concatenate([np.cos(turn), -np.sin(turn)], axis=1), jnp.bfloat16)
    share = np.where(np.arange(1, freqs + 1) == freqs, 1.0, 2.0)
    back = np.stack([np.cos(turn) * share, -np.sin(turn) * share], axis=0)
    back = jnp.asarray(back, jnp.bfloat16)

    gains = cal_gains.astype(jnp.float32) / 65536.0
    gains = gains.reshape(2, stations, group_count, CHUNKS, items)
    volts = voltages.reshape(2, stations, group_count, CHUNKS, items, time_count)
    groups = [list(range(half)), list(range(half, group_count))]
    arrived = []
    for k in range(CHUNKS):
        gain_real = gains[0, :, :, k, :, None]
        gain_imag = gains[1, :, :, k, :, None]
        volt_real = volts[0, :, :, k].astype(jnp.float32)
        volt_imag = volts[1, :, :, k].astype(jnp.float32)
        calibrated = jnp.stack(
            [
                volt_real * gain_real - volt_imag * gain_imag,
                volt_real * gain_imag + volt_imag * gain_real,
            ]
        ).astype(jnp.bfloat16)
        outgoing = jnp.transpose(calibrated, (2, 3, 0, 1, 4))
        outgoing = outgoing.reshape(group_count, items, 2 * stations, time_count)
        received = lax.all_to_all(outgoing, "chan", split_axis=0, concat_axis=0, tiled=True)
        spectra = detect_spectra(weights, table, received)
        arrived.append(
            lax.all_to_all(
                spectra, "chan", split_axis=0, concat_axis=0, tiled=True, axis_index_groups=groups
            )
        )
    picked = delays.reshape(trials, 2, half, CHUNKS, items)
    picked = lax.dynamic_index_in_dim(picked, own_half, axis=1, keepdims=False)
    order = jnp.transpose(picked, (0, 2, 1, 3)).reshape(trials, channels // 2)
    rotation = rotations(order, time_count)
    series = jnp.stack(arrived)
    series = series.reshape(channels // 2, 2, local_beams, 2, freqs)
    series = jnp.transpose(series, (1, 4, 2, 3, 0)).reshape(2, freqs, local_beams, channels)
    other = jnp.einsum("fbk,fkd->fbd", series[0], rotation, preferred_element_type=jnp.float32)
    pairs = [(i, (i + half) % group_count) for i in range(group_count)]
    incoming = lax.ppermute(other.astype(jnp.bfloat16), "chan", pairs)
    own = jnp.einsum("fbk,fkd->fbd", series[1], rotation, preferred_element_type=jnp.float32)
    total = (own + incoming.astype(jnp.float32)).astype(jnp.bfloat16)
    total = total.reshape(freqs, local_beams, 2, trials)
    result = jnp.einsum("fbpd,ptf->bdt", total, back, preferred_element_type=jnp.float32)
    return result * (1.0 / (time_count * math.sqrt(channels)))


def solution(mesh):
    return jax.shard_map(
        body,
        mesh=mesh,
        in_specs=(P(None, ("obs", "chan"), None, None), P(None, ("obs", "chan"), None), P(), P()),
        out_specs=P(("obs", "chan"), None, None),
        check_vma=False,
    )
```

```python
import functools
import math

import jax
import jax.numpy as jnp
import numpy as np
from jax import lax
from jax.experimental import pallas as pl
from jax.experimental.pallas import tpu as pltpu
from jax.sharding import PartitionSpec as P

PHASES = 1024
CHUNKS = 4


def beam_matrix(beam_phase, group_count, own_half):
    beam_count, station_count = beam_phase.shape
    half = group_count // 2
    local_beams = beam_count // group_count
    grid = beam_phase.reshape(2, half, local_beams, station_count)
    grid = jnp.where(own_half == 0, grid[::-1], grid)
    grid = jnp.transpose(grid, (1, 0, 2, 3)).reshape(beam_count, group_count, station_count // group_count)
    angles = grid.astype(jnp.float32) * (2.0 * math.pi / PHASES)
    scaling = 1.0 / math.sqrt(station_count)
    real_part = jnp.cos(angles) * scaling
    imag_part = jnp.sin(angles) * scaling
    upper_rows = jnp.stack([real_part, -imag_part], axis=2)
    bottom = jnp.stack([imag_part, real_part], axis=2)
    rows = jnp.concatenate([upper_rows, bottom], axis=0)
    return rows.reshape(2 * beam_count, 2 * station_count).astype(jnp.bfloat16)


def exchange_kernel(
    count, items, data_ref, weight_ref, table_ref, out_ref, held, spectra, send_in, recv_in, send_out, recv_out, local_in, local_out
):
    me = lax.axis_index("chan")
    half = count // 2
    first = me // half * half
    place = lax.rem(me, half)
    channels = data_ref.shape[1]
    chunks = channels // items
    beams = weight_ref.shape[0] // 2

    barrier = pltpu.get_barrier_semaphore()

    def greet(step, carry):
        pl.semaphore_signal(
            barrier, inc=1, device_id={"chan": lax.rem(me + step, count)}, device_id_type=pl.DeviceIdType.MESH
        )
        return carry

    lax.fori_loop(1, count, greet, 0)
    pl.semaphore_wait(barrier, count - 1)

    def inward(k, step):
        target = lax.rem(me + step, count)
        part = pl.ds(k * items, items)
        return pltpu.make_async_remote_copy(
            src_ref=data_ref.at[target, part],
            dst_ref=held.at[me, part],
            send_sem=send_in.at[k, step],
            recv_sem=recv_in.at[k, step],
            device_id={"chan": target},
            device_id_type=pl.DeviceIdType.MESH,
        )

    def outward(k, step):
        target = lax.rem(place + step, half)
        part = pl.ds(k * items, items)
        return pltpu.make_async_remote_copy(
            src_ref=spectra.at[target, part],
            dst_ref=out_ref.at[place, part],
            send_sem=send_out.at[k, step],
            recv_sem=recv_out.at[k, step],
            device_id={"chan": first + target},
            device_id_type=pl.DeviceIdType.MESH,
        )

    def each(start, stop, act):
        def run(step, carry):
            act(step)
            return carry

        lax.fori_loop(start, stop, run, 0)

    own = pltpu.make_async_copy(data_ref.at[me], held.at[me], local_in)
    ahead = 2
    for k in range(min(ahead, chunks)):
        each(1, count, lambda step: inward(k, step).start())
    own.start()
    own.wait()
    for k in range(chunks):
        each(1, count, lambda step: inward(k, step).wait_recv())
        if k + ahead < chunks:
            each(1, count, lambda step: inward(k + ahead, step).start())

        def channel(c):
            data = held[:, c].reshape(weight_ref.shape[1], held.shape[3])
            sums = jnp.dot(weight_ref[...], data, preferred_element_type=jnp.float32)
            powers = (sums[:beams] * sums[:beams] + sums[beams:] * sums[beams:]).astype(jnp.bfloat16)
            series = jnp.dot(powers, table_ref[...], preferred_element_type=jnp.float32)
            spectra[:, c] = series.astype(jnp.bfloat16).reshape(half, spectra.shape[2], spectra.shape[3])

        each(k * items, (k + 1) * items, channel)
        each(1, half, lambda step: outward(k, step).start())
    stay = pltpu.make_async_copy(spectra.at[place], out_ref.at[place], local_out)
    stay.start()
    stay.wait()
    for k in range(chunks):
        each(1, count, lambda step: inward(k, step).wait_send())
        each(1, half, lambda step: outward(k, step).wait())


def exchange(weights, table, data):
    count, channels, rows, time_count = data.shape
    beams = weights.shape[0] // 2
    half = count // 2
    found = (half, channels, beams // half, time_count)
    return pl.pallas_call(
        functools.partial(exchange_kernel, count, channels // CHUNKS),
        out_shape=jax.ShapeDtypeStruct(found, jnp.bfloat16),
        in_specs=[
            pl.BlockSpec(memory_space=pl.ANY),
            pl.BlockSpec(memory_space=pltpu.VMEM),
            pl.BlockSpec(memory_space=pltpu.VMEM),
        ],
        out_specs=pl.BlockSpec(memory_space=pl.ANY),
        scratch_shapes=[
            pltpu.VMEM(data.shape, jnp.bfloat16),
            pltpu.VMEM(found, jnp.bfloat16),
            pltpu.SemaphoreType.DMA((CHUNKS, count)),
            pltpu.SemaphoreType.DMA((CHUNKS, count)),
            pltpu.SemaphoreType.DMA((CHUNKS, half)),
            pltpu.SemaphoreType.DMA((CHUNKS, half)),
            pltpu.SemaphoreType.DMA,
            pltpu.SemaphoreType.DMA,
        ],
        compiler_params=pltpu.CompilerParams(
            collective_id=0, has_side_effects=True, vmem_limit_bytes=48 * 2**20
        ),
        cost_estimate=pl.CostEstimate(
            flops=2 * channels * time_count * (weights.size + beams * time_count),
            bytes_accessed=4 * data.size,
            transcendentals=0,
        ),
    )(data, weights, table)


def rotations(delays, time_count):
    freqs = time_count // 2
    low = min(16, freqs)
    high = freqs // low
    turned = delays.T

    def unit(multiples):
        level = multiples[:, None, None] * turned[None] % time_count
        angle = level.astype(jnp.float32) * (2.0 * math.pi / time_count)
        return jnp.cos(angle), jnp.sin(angle)

    low_cos, low_sin = unit(jnp.arange(1, low + 1, dtype=jnp.int32))
    high_cos, high_sin = unit(jnp.arange(high, dtype=jnp.int32) * low)
    cosine = high_cos[:, None] * low_cos[None] - high_sin[:, None] * low_sin[None]
    sine = high_cos[:, None] * low_sin[None] + high_sin[:, None] * low_cos[None]
    cosine = cosine.reshape((freqs,) + turned.shape).astype(jnp.bfloat16)
    sine = sine.reshape((freqs,) + turned.shape).astype(jnp.bfloat16)
    return jnp.concatenate([cosine, sine], axis=2)


def rotate(series, rotation, trials):
    channels, beams, samples = series.shape
    freqs = samples // 2
    series = series.reshape(channels, beams, 2, freqs)
    series = jnp.transpose(series, (3, 2, 1, 0)).reshape(freqs, 2 * beams, channels)
    parts = jnp.einsum("frk,fkd->frd", series, rotation, preferred_element_type=jnp.float32)
    real_part = parts[:, :beams, :trials] - parts[:, beams:, trials:]
    imag_part = parts[:, :beams, trials:] + parts[:, beams:, :trials]
    return jnp.concatenate([real_part, imag_part], axis=2)


def body(voltages, cal_gains, beam_phase, delays):
    group_count = lax.axis_size("chan")
    half = group_count // 2
    me = lax.axis_index("chan")
    own_half = me // half
    _, stations, channels, time_count = voltages.shape
    freqs = time_count // 2
    trials = delays.shape[0]
    local_beams = beam_phase.shape[0] // group_count

    weights = beam_matrix(beam_phase, group_count, own_half)
    turn = np.outer(np.arange(time_count), np.arange(1, freqs + 1)) % time_count
    turn = turn * (2.0 * np.pi / time_count)
    table = jnp.asarray(np.concatenate([np.cos(turn), -np.sin(turn)], axis=1), jnp.bfloat16)
    share = np.where(np.arange(1, freqs + 1) == freqs, 1.0, 2.0)
    back = np.stack([np.cos(turn) * share, -np.sin(turn) * share], axis=0)
    back = jnp.asarray(back, jnp.bfloat16)

    gains = cal_gains.astype(jnp.float32) / 65536.0
    gain_real = gains[0][:, :, None]
    gain_imag = gains[1][:, :, None]
    volt_real = voltages[0].astype(jnp.float32)
    volt_imag = voltages[1].astype(jnp.float32)
    calibrated = jnp.stack(
        [
            volt_real * gain_real - volt_imag * gain_imag,
            volt_real * gain_imag + volt_imag * gain_real,
        ]
    ).astype(jnp.bfloat16)
    outgoing = jnp.transpose(calibrated.reshape(2 * stations, channels, time_count), (1, 0, 2))
    outgoing = outgoing.reshape(group_count, channels // group_count, 2 * stations, time_count)
    arrived = exchange(weights, table, outgoing)

    order = delays.reshape(trials, 2, channels // 2)
    order = lax.dynamic_index_in_dim(order, own_half, axis=1, keepdims=False)
    rotation = rotations(order, time_count)
    series = arrived.reshape(channels // 2, 2 * local_beams, time_count)
    other = rotate(series[:, :local_beams], rotation, trials)
    pairs = [(i, (i + half) % group_count) for i in range(group_count)]
    incoming = lax.ppermute(other.astype(jnp.bfloat16), "chan", pairs)
    own = lax.optimization_barrier(rotate(series[:, local_beams:], rotation, trials))
    total = (own + incoming.astype(jnp.float32)).astype(jnp.bfloat16)
    total = total.reshape(freqs, local_beams, 2, trials)
    result = jnp.einsum("fbpd,ptf->bdt", total, back, preferred_element_type=jnp.float32)
    return result * (1.0 / (time_count * math.sqrt(channels)))


def solution(mesh):
    return jax.shard_map(
        body,
        mesh=mesh,
        in_specs=(P(None, ("obs", "chan"), None, None), P(None, ("obs", "chan"), None), P(), P()),
        out_specs=P(("obs", "chan"), None, None),
        check_vma=False,
    )
```
